256 devices in a mesh: row: 8 (over x, z_lo), col: 8 (over y, core), grid: 4 (over z_hi).
Axes of the slice: x: 4, y: 4, z: 8 (z_hi: 4, z_lo: 2; z = z_hi * 2 + z_lo), core: 2. Of those that a mesh axis runs over, the one named last changes fastest.
Arguments:
- snapshots: bfloat16 [16384, 1024], P(('row', 'col', 'grid')), may hold values from -6 to 6
- jitter_code: int32 [16384], replicated, may hold values from 0 to 63
- slab_start: int32 [4], P('grid'), may hold values from 0 to 127
- gamma: float32 [2048], P('grid'), may hold values from 0.1 to 10
- noise_var: float32 [1], replicated, may hold values from 0.3 to 1.5
Outputs:
- steered: float32 [16384, 2048], P(('row', 'col'), 'grid')
- gamma_new: float32 [2048], P('grid')
The draws below stay inside these ranges and needn't reach their ends.
All inputs are finite; a program needn't handle non-finite values.
Results may differ from the reference program's by a relative error of at most 0.0003.
Values may be sent and summed in bfloat16 or wider, within the bound.
No kernel may reach another device: no remote copies, remote signals or barrier semaphores. Data moves between devices by JAX's collectives and lax.ppermute only.
A program may use at most 64 MiB of HBM per device.

```python
import math
import jax
import jax.numpy as jnp
from jax import lax

M = 16384
SNAP = 1024
SLAB = 512
GRID = 65536
POINTS = 2048
N_GRID = 4


def set_ends(drawn, rng, least, largest):
    longest = drawn.shape.index(max(drawn.shape))
    spots = []
    for shift in (0, 1):
        where = [jax.random.randint(jax.random.fold_in(rng, axis), (), 0, length) for axis, length in enumerate(drawn.shape)]
        where[longest] = (where[longest] + shift) % drawn.shape[longest]
        spots.append(tuple(where))
    return drawn.at[spots[0]].set(least).at[spots[1]].set(largest)


def level_of(stream_key, dims, shards, least, top_value):
    factor_of, own = 1.0, jax.random.fold_in(stream_key, 6)
    for dim, shards_of in shards:
        heights = jnp.exp(jax.random.uniform(jax.random.fold_in(own, dim), (shards_of,), jnp.float32, least / len(shards), top_value / len(shards)))
        factor_of = factor_of * jnp.repeat(heights, dims[dim] // shards_of).reshape([-1 if axis == dim else 1 for axis in range(len(dims))])
    return factor_of


def bell_draw(key, shape, width, most, cuts=(), kind=jnp.bfloat16):
    gain = level_of(key, shape, cuts, -0.22, 0.18) if cuts else 1.0
    array = jax.random.normal(key, shape, jnp.float32) * width * gain
    return jnp.minimum(jnp.maximum(array, -most), most).astype(kind)


def setup_inputs(seed: int = 0) -> dict:
    keys = jax.random.split(jax.random.key(seed), 6)
    snapshots = bell_draw(keys[0], (M, SNAP), 1.0, 6.0, ((0, 256),))
    jitter_code = set_ends(jax.random.randint(keys[1], (M,), 0, 64), jax.random.fold_in(keys[1], 1), 0, 63).astype(jnp.int32)
    slab_start = set_ends(jax.random.randint(keys[2], (N_GRID,), 0, GRID // SLAB), jax.random.fold_in(keys[2], 1), 0, (GRID // SLAB) - 1).astype(jnp.int32)
    gamma = jnp.clip(jnp.exp(math.log(10.0) - 4.6051702 * jax.random.uniform(keys[3], (POINTS,), jnp.float32) ** level_of(keys[3], (POINTS,), ((0, 4),), -0.2, 0.2)), 0.1, 10.0)
    noise_var = jnp.clip(jax.random.uniform(keys[4], (1,), jnp.float32, 0.3, 1.5), 0.3, 1.5)
    return dict(snapshots=snapshots, jitter_code=jitter_code, slab_start=slab_start, gamma=gamma, noise_var=noise_var)


def steer(sensor, codes, points):
    pos = (64 * sensor + codes + 32).astype(jnp.int32)[:, None]
    low = (points % 256).astype(jnp.int32)[None, :]
    high = (points // 256).astype(jnp.int32)[None, :]
    modulus = 64 * GRID
    first = (pos * low) % modulus
    second = ((pos * high) % (modulus // 256)) * 256
    wound = (first + second) % modulus
    turns = wound.astype(jnp.float32) / modulus - (pos % 128).astype(jnp.float32) / 128.0
    return jnp.cos(2.0 * jnp.pi * turns)


def reference(snapshots, jitter_code, slab_start, gamma, noise_var):
    sensors = jnp.arange(M, dtype=jnp.int32)
    stride = GRID // SLAB
    points = (slab_start[:, None] + stride * jnp.arange(SLAB, dtype=jnp.int32)[None, :]).reshape(-1).astype(jnp.int32)
    steering = steer(sensors, jitter_code, points)
    data = snapshots.astype(jnp.float32)
    projected = jnp.dot(data.T, steering, precision=lax.Precision.HIGHEST)
    steered = jnp.dot(data, projected, precision=lax.Precision.HIGHEST) / SNAP
    forms = jnp.sum(steering * steered, axis=0)
    norms = jnp.sum(steering * steering, axis=0)
    gamma_new = gamma * forms / (norms * (gamma + noise_var[0]))
    return steered, gamma_new
```

```python
import jax
import jax.numpy as jnp
import numpy as np
from jax import lax
from jax.experimental import pallas as pl
from jax.experimental.pallas import tpu as pltpu
from jax.sharding import Mesh, PartitionSpec as P

SNAP = 1024
PLANE = ("x", "zl", "y")


def fit_sine():
    v = np.cos(np.linspace(0.0, np.pi, 4001)) * 0.25
    basis = np.stack([v ** (2 * i + 1) for i in range(6)], axis=1)
    return tuple(float(c) for c in np.linalg.lstsq(basis, np.sin(2 * np.pi * v), rcond=None)[0])


COEF = fit_sine()


def sine_poly(v):
    w = v * v
    total = jnp.float32(COEF[5])
    for c in COEF[4::-1]:
        total = total * w + jnp.float32(c)
    return total * v


def cos_sin(angle):
    turns = (angle << 10).astype(jnp.float32) * jnp.float32(2.0**-32)
    size = jnp.abs(turns)
    v = size - 0.25
    cosine = -sine_poly(v)
    sine = sine_poly(0.25 - jnp.abs(v))
    return cosine, jnp.where(turns < 0, -sine, sine)


def split(x):
    high = x.astype(jnp.bfloat16)
    return high, (x - high.astype(jnp.float32)).astype(jnp.bfloat16)


def arrange_kernel(core_ref, mine_ref, other_ref, out_ref):
    mine = mine_ref[...].astype(jnp.float32)
    other = other_ref[...].astype(jnp.float32)
    first = core_ref[0] == 0
    both = jnp.concatenate([jnp.where(first, mine, other), jnp.where(first, other, mine)], axis=0)
    out_ref[...] = both.T.astype(jnp.bfloat16)


def partial_kernel(scalars, jit_ref, data_ref, t1, t2, t3, out_ref, acc, table, left_hi, left_lo):
    g = scalars[1]
    sub = lax.broadcasted_iota(jnp.int32, (8, 128), 0)
    sub16 = lax.broadcasted_iota(jnp.int32, (16, 128), 0)
    lane = lax.broadcasted_iota(jnp.int32, (8, 128), 1)
    start = jnp.full((8, 128), scalars[0], jnp.int32)
    for slot, ref in enumerate((t1, t2, t3)):
        theirs = ref[64:80, 0:128].astype(jnp.float32).astype(jnp.int32)[0:8]
        start = jnp.where(sub % 4 == slot + 1, theirs, start)
    double = jnp.where(sub < 4, 1, 2)
    place = (lane // 64) * 256 + (lane % 64) + g * 64

    def block(b, carry):
        for part in range(4):
            q = b * 4 + part
            codes = jit_ref[pl.ds(q, 1), :]
            pos = (q * 512 + place) * 64 + codes + 32
            offset = (pos & 127) << 15
            pos16 = jnp.concatenate([pos, pos], axis=0)
            c, s = cos_sin(pos16 * (sub16 * 128))
            cstep, sstep = cos_sin(pos * 2048)
            cstep = jnp.concatenate([cstep, cstep], axis=0)
            sstep = jnp.concatenate([sstep, sstep], axis=0)
            lanes = slice(part * 128, part * 128 + 128)
            lanes_s = slice(512 + part * 128, 512 + part * 128 + 128)
            for step in range(8):
                rows = slice(step * 16, step * 16 + 16)
                rows_lo = slice(128 + step * 16, 128 + step * 16 + 16)
                hi, lo = split(c)
                table[rows, lanes] = hi
                table[rows_lo, lanes] = lo
                hi, lo = split(s)
                table[rows, lanes_s] = hi
                table[rows_lo, lanes_s] = lo
                if step < 7:
                    c, s = c * cstep - s * sstep, s * cstep + c * sstep
            cc, sc = cos_sin(pos * (sub * 16384))
            ca, sa = cos_sin((pos * start - offset) * double)
            data = data_ref[pl.ds(q * 16, 16), :].astype(jnp.float32)
            for slot in range(4):
                ra, rs = ca[slot : slot + 1], sa[slot : slot + 1]
                fc = ra * cc - rs * sc
                fs = -(rs * cc + ra * sc)
                for jh in range(4):
                    rows = slice((jh * 4 + slot) * 16, (jh * 4 + slot) * 16 + 16)
                    hi, lo = split(data * fc[jh : jh + 1])
                    left_hi[rows, lanes] = hi
                    left_lo[rows, lanes] = lo
                    hi, lo = split(data * fs[jh : jh + 1])
                    left_hi[rows, lanes_s] = hi
                    left_lo[rows, lanes_s] = lo
            for pair in range(2):
                fcs, fss = [], []
                for slot in (2 * pair, 2 * pair + 1):
                    ra, rs = ca[4 + slot : 5 + slot], sa[4 + slot : 5 + slot]
                    fcs.append(ra * cc - rs * sc)
                    fss.append(-(rs * cc + ra * sc))
                rows = slice(256 + pair * 16, 256 + pair * 16 + 16)
                hi, lo = split(jnp.concatenate(fcs, axis=0))
                left_hi[rows, lanes] = hi
                left_lo[rows, lanes] = lo
                hi, lo = split(jnp.concatenate(fss, axis=0))
                left_hi[rows, lanes_s] = hi
                left_lo[rows, lanes_s] = lo
        right = table[...]
        dims = (((1,), (1,)), ((), ()))
        acc[...] += lax.dot_general(left_hi[...], right, dims, preferred_element_type=jnp.float32) + lax.dot_general(
            left_lo[...], right, dims, preferred_element_type=jnp.float32
        )
        return carry

    acc[...] = jnp.zeros_like(acc)
    lax.fori_loop(0, 8, block, 0)
    for slot in range(4):
        dest = lax.rem(g + slot, 4)
        for jh in range(4):
            lanes = slice(jh * 128, jh * 128 + 128)
            r = (jh * 4 + slot) * 16
            out_ref[dest, 0:16, lanes] = acc[r : r + 16, 0:128] + acc[r : r + 16, 128:256]
            low = 256 + slot * 8 + jh
            pair = [acc[i : i + 1, 0:128] + acc[i : i + 1, 128:256] for i in (low, low + 4)]
            out_ref[dest, 16:24, lanes] = jnp.concatenate(pair + [jnp.zeros((6, 128), jnp.float32)], axis=0)


def code_kernel(parts_ref, out_ref, norm_ref):
    total = (parts_ref[0] + parts_ref[1]) + (parts_ref[2] + parts_ref[3])
    piece = total[0:16]
    norm_ref[...] = total[16:24]
    most = jnp.max(jnp.abs(piece), axis=1, keepdims=True)
    power = jnp.ceil(jnp.log2(jnp.maximum(most, 2.0**-60)))
    mantissa = jnp.ceil(most * jnp.exp2(-power) * 16384.0) + 1.0
    unit = mantissa * jnp.exp2(power) * (1.0 / (16384.0 * 32767.0))
    code = jnp.round(piece * (1.0 / unit))
    lane = lax.broadcasted_iota(jnp.int32, (16, 128), 1)
    scale = jnp.where(lane == 0, mantissa, power)
    whole = jnp.concatenate([code, scale], axis=1).astype(jnp.int32).astype(jnp.int16)
    for q in range(32):
        out_ref[q] = whole


def decode(ref):
    scale = ref[:, 512:640].astype(jnp.int32).astype(jnp.float32)
    unit = scale[:, 0:1] * jnp.exp2(scale[:, 1:2]) * (1.0 / (16384.0 * 32767.0))
    return ref[:, 0:512].astype(jnp.int32).astype(jnp.float32) * unit


def final_kernel(scalars, own_ref, other_ref, d0, d1, d2, d3, norm_ref, gamma_ref, noise_ref, out_ref, gamma_out):
    core = scalars[0]
    g = scalars[1]
    p_own = decode(own_ref)
    p_oth = decode(other_ref)
    first = core == 0
    forms = jnp.zeros((1, 512), jnp.float32)
    highs, lows = [], []
    for p in (p_own, p_oth):
        forms = forms + jnp.sum(p * p, axis=0, keepdims=True)
        hi, lo = split(p * (1.0 / SNAP))
        highs.append(hi)
        lows.append(lo)
    for slot, ref in enumerate((d0, d1, d2, d3)):
        left = ref[0:64, 0:512]
        right = ref[0:64, 512:1024]
        mine = jnp.where(first, left, right)
        theirs = jnp.where(first, right, left)
        total = jnp.zeros((64, 512), jnp.float32)
        for data, hi, lo in ((mine, highs[0], lows[0]), (theirs, highs[1], lows[1])):
            total = total + jnp.dot(data, hi, preferred_element_type=jnp.float32)
            total = total + jnp.dot(data, lo, preferred_element_type=jnp.float32)
        rows = pl.multiple_of(lax.rem(g + slot, 4) * 64, 64)
        out_ref[pl.ds(rows, 64), :] = total
    pick = jnp.where(
        lax.broadcasted_iota(jnp.int32, (512, 256), 0) == 2 * lax.broadcasted_iota(jnp.int32, (512, 256), 1), 1.0, 0.0
    ).astype(jnp.float32)
    even = jnp.dot(norm_ref[...], pick, precision=lax.Precision.HIGHEST, preferred_element_type=jnp.float32)
    norms = 8192.0 + 0.5 * jnp.concatenate([even[0:1], even[1:2]], axis=1)
    gamma = gamma_ref[...]
    gamma_out[...] = gamma * (forms * (1.0 / SNAP)) / (norms * (gamma + noise_ref[0]))


VMEM = pl.BlockSpec(memory_space=pltpu.VMEM)
SMEM = pl.BlockSpec(memory_space=pltpu.SMEM)


def params(mib=48):
    return pltpu.CompilerParams(vmem_limit_bytes=mib * 2**20)


def on_device(snapshots, jitter_code, slab_start, gamma, noise_var):
    core = lax.axis_index("core")
    g = lax.axis_index("grid")

    def turn(x, shift):
        return lax.ppermute(x, "grid", [((i + shift) % 4, i) for i in range(4)])

    tagged = jnp.concatenate([snapshots, jnp.full((16, 1024), slab_start[0].astype(jnp.bfloat16))], axis=0)
    turned_rows = [turn(tagged, s) for s in (1, 2, 3)]
    mine = lax.dynamic_slice(snapshots, (0, core * 512), (64, 512))
    give = lax.dynamic_slice(snapshots, (0, (1 - core) * 512), (64, 512))
    other = lax.ppermute(give, "core", [(0, 1), (1, 0)])
    scalars = jnp.stack([slab_start[0], g.astype(jnp.int32)])
    codes = lax.dynamic_slice(jitter_code.reshape(64, 256), (0, g * 64), (64, 64)).reshape(32, 128)
    turned = pl.pallas_call(
        arrange_kernel,
        out_shape=jax.ShapeDtypeStruct((512, 128), jnp.bfloat16),
        in_specs=[SMEM, VMEM, VMEM],
        out_specs=VMEM,
        name="arrange",
    )(core[None].astype(jnp.int32), mine, other)
    mixed = lax.all_to_all(turned.reshape(32, 16, 128), PLANE, 0, 0, tiled=True)
    mixed, turned_rows = lax.optimization_barrier((mixed, turned_rows))
    rows = [snapshots] + turned_rows
    part = pl.pallas_call(
        partial_kernel,
        out_shape=jax.ShapeDtypeStruct((4, 24, 512), jnp.float32),
        in_specs=[SMEM] + [VMEM] * 5,
        out_specs=VMEM,
        scratch_shapes=[
            pltpu.VMEM((288, 256), jnp.float32),
            pltpu.VMEM((256, 1024), jnp.bfloat16),
            pltpu.VMEM((288, 1024), jnp.bfloat16),
            pltpu.VMEM((288, 1024), jnp.bfloat16),
        ],
        compiler_params=params(),
        name="partial",
    )(scalars, codes, mixed.reshape(512, 128), *turned_rows)
    parts = lax.all_to_all(part, "grid", 0, 0, tiled=True)
    coded, norm = pl.pallas_call(
        code_kernel,
        out_shape=(jax.ShapeDtypeStruct((32, 16, 640), jnp.int16), jax.ShapeDtypeStruct((8, 512), jnp.float32)),
        in_specs=[VMEM],
        out_specs=(VMEM, VMEM),
        name="code",
    )(parts)
    half = lax.all_to_all(coded, PLANE, 0, 0, tiled=True).reshape(512, 640)
    half_other = lax.ppermute(half, "core", [(0, 1), (1, 0)])
    steered, gamma_new = pl.pallas_call(
        final_kernel,
        out_shape=(jax.ShapeDtypeStruct((256, 512), jnp.float32), jax.ShapeDtypeStruct((1, 512), jnp.float32)),
        in_specs=[SMEM] + [VMEM] * 8 + [SMEM],
        out_specs=(VMEM, VMEM),
        compiler_params=params(),
        name="final",
    )(
        jnp.stack([core, g]).astype(jnp.int32),
        half,
        half_other,
        *rows,
        norm,
        gamma.reshape(1, 512),
        noise_var,
    )
    return steered, gamma_new.reshape(512)


def solution(mesh):
    fine = Mesh(mesh.devices.reshape(4, 2, 4, 2, 4), ("x", "zl", "y", "core", "grid"))
    sensors = ("x", "zl", "y", "core")
    in_specs = (P((*sensors, "grid"), None), P(), P("grid"), P("grid"), P())
    out_specs = (P(sensors, "grid"), P("grid"))
    return jax.shard_map(on_device, mesh=fine, in_specs=in_specs, out_specs=out_specs, check_vma=False)
```

```python
import jax
import jax.numpy as jnp
import numpy as np
from jax import lax
from jax.experimental import pallas as pl
from jax.experimental.pallas import tpu as pltpu
from jax.sharding import Mesh, PartitionSpec as P

SNAP = 1024
PLANE = ("x", "zl", "y")


def fit_sine():
    v = np.cos(np.linspace(0.0, np.pi, 4001)) * 0.25
    basis = np.stack([v ** (2 * i + 1) for i in range(6)], axis=1)
    return tuple(float(c) for c in np.linalg.lstsq(basis, np.sin(2 * np.pi * v), rcond=None)[0])


COEF = fit_sine()


def sine_poly(v):
    w = v * v
    total = jnp.float32(COEF[5])
    for c in COEF[4::-1]:
        total = total * w + jnp.float32(c)
    return total * v


def cos_sin(angle):
    turns = (angle << 10).astype(jnp.float32) * jnp.float32(2.0**-32)
    size = jnp.abs(turns)
    v = size - 0.25
    cosine = -sine_poly(v)
    sine = sine_poly(0.25 - jnp.abs(v))
    return cosine, jnp.where(turns < 0, -sine, sine)


def split(x):
    high = x.astype(jnp.bfloat16)
    return high, (x - high.astype(jnp.float32)).astype(jnp.bfloat16)


def table_kernel(scalars, jit_ref, table_out, factor_ref, norm_ref, table_ref, left, acc, sems):
    sub = lax.broadcasted_iota(jnp.int32, (8, 128), 0)
    lane = lax.broadcasted_iota(jnp.int32, (8, 128), 1)
    start = jnp.where(sub == 0, scalars[1], jnp.where(sub == 1, 1024, 2048))
    keep = jnp.where(sub == 0, 1 << 15, 0)
    place = lane + scalars[0] * 256
    dims = (((1,), (1,)), ((), ()))

    def store(b):
        return pltpu.make_async_copy(table_ref.at[b], table_out.at[b], sems.at[b])

    def block(b, carry):
        for part in range(4):
            q = b * 2 + part // 2
            cols = slice(part % 2 * 128, part % 2 * 128 + 128)
            pos = (q * 512 + place + part % 2 * 128) * 64 + jit_ref[pl.ds(q * 4 + scalars[0] * 2 + part % 2, 1), :] + 32
            c, s = cos_sin(pos * (sub * 128))
            cc, sc = cos_sin(pos * (sub * 16384))
            ca, sa = cos_sin(pos * start - (pos & 127) * keep)
            c8, s8, c16, s16 = ca[1:2], sa[1:2], ca[2:3], sa[2:3]
            c, s = jnp.concatenate([c, c * c8 - s * s8], axis=0), jnp.concatenate([s, s * c8 + c * s8], axis=0)
            lanes = slice(part * 128, part * 128 + 128)
            lanes_s = slice(512 + part * 128, 512 + part * 128 + 128)
            for step in range(8):
                rows = slice(step * 16, step * 16 + 16)
                rows_lo = slice(128 + step * 16, 128 + step * 16 + 16)
                hi, lo = split(c)
                table_ref[b, rows, lanes] = hi
                table_ref[b, rows_lo, lanes] = lo
                hi, lo = split(s)
                table_ref[b, rows, lanes_s] = hi
                table_ref[b, rows_lo, lanes_s] = lo
                if step < 7:
                    c, s = c * c16 - s * s16, s * c16 + c * s16
            ra, rs = ca[0:1], sa[0:1]
            fc = ra * cc - rs * sc
            fs = -(rs * cc + ra * sc)
            factor_ref[q, :, cols] = jnp.where(sub < 4, fc, jnp.concatenate([fs[4:8], fs[0:4]], axis=0))
            r2, s2 = 2.0 * ra * ra - 1.0, 2.0 * ra * rs
            hi, lo = split(r2 * cc - s2 * sc)
            left[:, lanes] = jnp.concatenate([hi.astype(jnp.float32), lo.astype(jnp.float32)], axis=0).astype(jnp.bfloat16)
            hi, lo = split(-(s2 * cc + r2 * sc))
            left[:, lanes_s] = jnp.concatenate([hi.astype(jnp.float32), lo.astype(jnp.float32)], axis=0).astype(jnp.bfloat16)
        store(b).start()
        acc[...] += lax.dot_general(left[...], table_ref[b], dims, preferred_element_type=jnp.float32)
        return carry

    acc[...] = jnp.zeros_like(acc)
    lax.fori_loop(0, 16, block, 0)
    for b in range(16):
        store(b).wait()
    sums = (acc[0:8, 0:128] + acc[0:8, 128:256]) + (acc[8:16, 0:128] + acc[8:16, 128:256])
    for jh in range(4):
        pair = [sums[jh : jh + 1], sums[jh + 4 : jh + 5], jnp.zeros((6, 128), jnp.float32)]
        norm_ref[:, jh * 128 : jh * 128 + 128] = jnp.concatenate(pair, axis=0)


def arrange_kernel(scalars, d0, d1, d2, d3, out_ref, rows_ref, rows):
    g = scalars[0]
    for slot, ref in enumerate((d0, d1, d2, d3)):
        rows[pl.ds(pl.multiple_of(lax.rem(g + slot, 4) * 64, 64), 64), :] = ref[...]
    rows_ref[...] = rows[...]
    for half in range(2):
        turned = rows[:, half * 512 : half * 512 + 512].astype(jnp.float32).T.astype(jnp.bfloat16)
        out_ref[:, half * 16 : half * 16 + 16, :] = turned.reshape(32, 16, 256)


def partial_kernel(scalars, data_ref, table_in, factor_ref, norm_ref, keep_ref, give_ref, acc, left0, left1, table_ref, sems):
    dims = (((1,), (1,)), ((), ()))

    def fetch(b):
        return pltpu.make_async_copy(table_in.at[b], table_ref.at[b], sems.at[b])

    for b in range(16):
        fetch(b).start()

    def generate(b, left):
        for part in range(4):
            q = b * 2 + part // 2
            cols = slice(part % 2 * 128, part % 2 * 128 + 128)
            data = data_ref[q, :, cols].astype(jnp.float32)
            lanes = slice(part * 128, part * 128 + 128)
            lanes_s = slice(512 + part * 128, 512 + part * 128 + 128)
            for jh in range(4):
                rows = slice(jh * 32, jh * 32 + 32)
                rows_lo = slice(128 + jh * 32, 128 + jh * 32 + 32)
                hi, lo = split(data * factor_ref[q, jh : jh + 1, cols])
                left[rows, lanes] = hi
                left[rows_lo, lanes] = lo
                hi, lo = split(data * factor_ref[q, 4 + jh : 5 + jh, cols])
                left[rows, lanes_s] = hi
                left[rows_lo, lanes_s] = lo

    def multiply(b, left):
        acc[...] += lax.dot_general(left[...], table_ref[b], dims, preferred_element_type=jnp.float32)

    acc[...] = jnp.zeros_like(acc)
    generate(0, left0)

    def block(i, carry):
        generate(2 * i + 1, left1)
        multiply(2 * i, left0)
        generate(2 * i + 2, left0)
        multiply(2 * i + 1, left1)
        return carry

    for segment, ends in enumerate(((0, 1), (1, 3), (3, 5), (5, 7))):
        for b in range(4 * segment, 4 * segment + 4):
            fetch(b).wait()
        lax.fori_loop(*ends, block, 0)
    generate(15, left1)
    multiply(14, left0)
    multiply(15, left1)
    first = scalars[0] == 0
    for jh in range(4):
        lanes = slice(jh * 128, jh * 128 + 128)
        row = slice(jh * 32, jh * 32 + 32)
        row_lo = slice(128 + jh * 32, 128 + jh * 32 + 32)
        both = (acc[row, 0:128] + acc[row, 128:256]) + (acc[row_lo, 0:128] + acc[row_lo, 128:256])
        keep_ref[0:16, lanes] = jnp.where(first, both[0:16], both[16:32])
        give_ref[0:16, lanes] = jnp.where(first, both[16:32], both[0:16])
    keep_ref[16:24] = norm_ref[...]
    give_ref[16:24] = norm_ref[...]


def code_kernel(keep_ref, other_ref, out_ref, norm_ref):
    total = keep_ref[...] + other_ref[...]
    piece = total[0:16]
    norm_ref[...] = total[16:24]
    most = jnp.max(jnp.abs(piece), axis=1, keepdims=True)
    power = jnp.ceil(jnp.log2(jnp.maximum(most, 2.0**-60)))
    mantissa = jnp.ceil(most * jnp.exp2(-power) * 16384.0) + 1.0
    unit = mantissa * jnp.exp2(power) * (1.0 / (16384.0 * 32767.0))
    code = jnp.round(piece * (1.0 / unit))
    lane = lax.broadcasted_iota(jnp.int32, (16, 128), 1)
    scale = jnp.where(lane == 0, mantissa, power)
    whole = jnp.concatenate([code, scale], axis=1).astype(jnp.int32).astype(jnp.int16)
    for q in range(32):
        out_ref[q] = whole


def decode(ref):
    scale = ref[:, 512:640].astype(jnp.int32).astype(jnp.float32)
    unit = scale[:, 0:1] * jnp.exp2(scale[:, 1:2]) * (1.0 / (16384.0 * 32767.0))
    return ref[:, 0:512].astype(jnp.int32).astype(jnp.float32) * unit


def norm_kernel(norm_ref, gamma_ref, noise_ref, out_ref):
    pick = jnp.where(
        lax.broadcasted_iota(jnp.int32, (512, 256), 0) == 2 * lax.broadcasted_iota(jnp.int32, (512, 256), 1), 1.0, 0.0
    ).astype(jnp.float32)
    even = jnp.dot(norm_ref[...], pick, precision=lax.Precision.HIGHEST, preferred_element_type=jnp.float32)
    norms = 8192.0 + 0.5 * jnp.concatenate([even[0:1], even[1:2]], axis=1)
    gamma = gamma_ref[...]
    out_ref[...] = gamma * (1.0 / SNAP) / (norms * (gamma + noise_ref[0]))


def final_kernel(scalars, own_ref, other_ref, data, weight_ref, out_ref, gamma_out, high, low):
    core = scalars[0]
    forms = jnp.zeros((1, 512), jnp.float32)
    for half, ref in ((core, own_ref), (1 - core, other_ref)):
        p = decode(ref)
        forms = forms + jnp.sum(p * p, axis=0, keepdims=True)
        hi, lo = split(p * (1.0 / SNAP))
        rows = pl.ds(pl.multiple_of(half * 512, 512), 512)
        high[rows, :] = hi
        low[rows, :] = lo
    out_ref[...] = jnp.dot(data[...], high[...], preferred_element_type=jnp.float32) + jnp.dot(
        data[...], low[...], preferred_element_type=jnp.float32
    )
    gamma_out[...] = forms * weight_ref[...]


VMEM = pl.BlockSpec(memory_space=pltpu.VMEM)
SMEM = pl.BlockSpec(memory_space=pltpu.SMEM)
HBM = pl.BlockSpec(memory_space=pltpu.HBM)


def call(kernel, name, mib, outs, in_specs, scratch=(), cost=None, out_specs=None):
    return pl.pallas_call(
        kernel,
        out_shape=tuple(jax.ShapeDtypeStruct(*o) for o in outs),
        in_specs=in_specs,
        out_specs=out_specs or (VMEM,) * len(outs),
        scratch_shapes=scratch,
        compiler_params=pltpu.CompilerParams(vmem_limit_bytes=mib * 2**20),
        cost_estimate=cost,
        name=name,
    )


def on_device(snapshots, jitter_code, slab_start, gamma, noise_var):
    core = lax.axis_index("core").astype(jnp.int32)
    g = lax.axis_index("grid").astype(jnp.int32)
    swap = [(0, 1), (1, 0)]
    f32 = jnp.float32
    slots = [lax.ppermute(snapshots, "grid", [((i + s) % 4, i) for i in range(4)]) for s in (1, 2, 3)]
    bf16 = jnp.bfloat16
    dma = pltpu.SemaphoreType.DMA((16,))
    table, factor, norm_part = call(
        table_kernel,
        "table",
        48,
        [((16, 256, 1024), bf16), ((32, 8, 256), f32), ((8, 512), f32)],
        [SMEM, VMEM],
        [pltpu.VMEM((16, 256, 1024), bf16), pltpu.VMEM((16, 1024), bf16), pltpu.VMEM((16, 256), f32), dma],
        pl.CostEstimate(flops=12 * 10**9, bytes_accessed=10**7, transcendentals=0),
        (HBM, VMEM, VMEM),
    )(jnp.stack([core, slab_start[0]]), jitter_code.reshape(128, 128))
    table, slots = lax.optimization_barrier((table, slots))
    turned, rows = call(
        arrange_kernel,
        "arrange",
        8,
        [((32, 32, 256), bf16), ((256, 1024), bf16)],
        [SMEM] + [VMEM] * 4,
        [pltpu.VMEM((256, 1024), bf16)],
    )(g[None], snapshots, *slots)
    mixed = lax.all_to_all(turned, PLANE, 0, 0, tiled=True)
    keep, give = call(
        partial_kernel,
        "partial",
        48,
        [((24, 512), f32), ((24, 512), f32)],
        [SMEM, VMEM, HBM, VMEM, VMEM],
        [pltpu.VMEM((256, 256), f32)]
        + [pltpu.VMEM((256, 1024), bf16)] * 2
        + [pltpu.VMEM((16, 256, 1024), bf16), dma],
    )(core[None], mixed, table, factor, norm_part)
    coded, norm = call(code_kernel, "code", 8, [((32, 16, 640), jnp.int16), ((8, 512), f32)], [VMEM, VMEM])(
        keep, lax.ppermute(give, "core", swap)
    )
    half = lax.all_to_all(coded, PLANE, 0, 0, tiled=True).reshape(512, 640)
    half_other = lax.ppermute(half, "core", swap)
    (weight,) = call(norm_kernel, "weight", 8, [((1, 512), f32)], [VMEM, VMEM, SMEM])(
        norm, gamma.reshape(1, 512), noise_var
    )
    steered, gamma_new = call(
        final_kernel,
        "final",
        16,
        [((256, 512), f32), ((1, 512), f32)],
        [SMEM] + [VMEM] * 4,
        [pltpu.VMEM((1024, 512), bf16)] * 2,
    )(core[None], half, half_other, rows, weight)
    return steered, gamma_new.reshape(512)


def solution(mesh):
    fine = Mesh(mesh.devices.reshape(4, 2, 4, 2, 4), ("x", "zl", "y", "core", "grid"))
    sensors = ("x", "zl", "y", "core")
    in_specs = (P((*sensors, "grid"), None), P(), P("grid"), P("grid"), P())
    out_specs = (P(sensors, "grid"), P("grid"))
    return jax.shard_map(on_device, mesh=fine, in_specs=in_specs, out_specs=out_specs, check_vma=False)
```

```python
import jax
import jax.numpy as jnp
import numpy as np
from jax import lax
from jax.experimental import pallas as pl
from jax.experimental.pallas import tpu as pltpu
from jax.sharding import Mesh, PartitionSpec as P

SNAP = 1024
PLANE = ("x", "zl", "y")
NORM_STEPS = 127.9


def fit_sine():
    v = np.cos(np.linspace(0.0, np.pi, 4001)) * 0.25
    basis = np.stack([v ** (2 * i + 1) for i in range(6)], axis=1)
    return tuple(float(c) for c in np.linalg.lstsq(basis, np.sin(2 * np.pi * v), rcond=None)[0])


COEF = fit_sine()


def sine_poly(v):
    w = v * v
    total = jnp.float32(COEF[5])
    for c in COEF[4::-1]:
        total = total * w + jnp.float32(c)
    return total * v


def cos_sin(angle):
    turns = (angle << 10).astype(jnp.float32) * jnp.float32(2.0**-32)
    size = jnp.abs(turns)
    v = size - 0.25
    cosine = -sine_poly(v)
    sine = sine_poly(0.25 - jnp.abs(v))
    return cosine, jnp.where(turns < 0, -sine, sine)


def split(x):
    high = x.astype(jnp.bfloat16)
    return high, (x - high.astype(jnp.float32)).astype(jnp.bfloat16)


def angles(scalars, start_row):
    sub = lax.broadcasted_iota(jnp.int32, (8, 128), 0)
    lane = lax.broadcasted_iota(jnp.int32, (8, 128), 1)
    start = jnp.where(sub == 0, start_row, jnp.where(sub == 1, 1024, 2048))
    return sub, lane + scalars[0] * 256, start, jnp.where(sub == 0, 1 << 15, 0)


def fill_table(pos, constants, table, lanes, lanes_s):
    sub, _, start, keep = constants
    c, s = cos_sin(pos * (sub * 128))
    cc, sc = cos_sin(pos * (sub * 16384))
    ca, sa = cos_sin(pos * start - (pos & 127) * keep)
    c8, s8, c16, s16 = ca[1:2], sa[1:2], ca[2:3], sa[2:3]
    c, s = jnp.concatenate([c, c * c8 - s * s8], axis=0), jnp.concatenate([s, s * c8 + c * s8], axis=0)
    for step in range(8):
        rows = slice(step * 16, step * 16 + 16)
        rows_lo = slice(128 + step * 16, 128 + step * 16 + 16)
        table[rows, lanes], table[rows_lo, lanes] = split(c)
        table[rows, lanes_s], table[rows_lo, lanes_s] = split(s)
        if step < 7:
            c, s = c * c16 - s * s16, s * c16 + c * s16
    return cc, sc, ca[0:1], sa[0:1]


def table_kernel(scalars, jit_ref, rows_ref, table_out, factor_ref, own_ref, table_ref, sems):
    own_ref[...] = rows_ref[...]
    constants = angles(scalars, scalars[1])

    def store(b):
        return pltpu.make_async_copy(table_ref.at[b], table_out.at[b], sems.at[b])

    def block(b, carry):
        for part in range(4):
            q = b * 2 + part // 2
            half = part % 2
            cols = slice(half * 128, half * 128 + 128)
            pos = (q * 512 + constants[1] + half * 128) * 64 + jit_ref[pl.ds(q * 4 + scalars[0] * 2 + half, 1), :] + 32
            lanes = slice(part * 128, part * 128 + 128)
            lanes_s = slice(512 + part * 128, 512 + part * 128 + 128)
            cc, sc, ra, rs = fill_table(pos, constants, table_ref.at[b], lanes, lanes_s)
            fc, fs = ra * cc - rs * sc, -(rs * cc + ra * sc)
            factor_ref[q, :, cols] = jnp.concatenate([fc[0:4], fs[0:4]], axis=0)
        store(b).start()
        return carry

    lax.fori_loop(0, 16, block, 0)
    for b in range(16):
        store(b).wait()


def norm_kernel(scalars, jit_ref, out_ref, table, left):
    constants = angles(scalars, scalars[1])
    q = scalars[2]
    for part in range(2):
        pos = (q * 512 + constants[1] + part * 128) * 64 + jit_ref[pl.ds(q * 4 + scalars[0] * 2 + part, 1), :] + 32
        lanes = slice(part * 128, part * 128 + 128)
        lanes_s = slice(256 + part * 128, 256 + part * 128 + 128)
        cc, sc, ra, rs = fill_table(pos, constants, table, lanes, lanes_s)
        r2, s2 = 2.0 * ra * ra - 1.0, 2.0 * ra * rs
        for value, where in ((r2 * cc - s2 * sc, lanes), (-(s2 * cc + r2 * sc), lanes_s)):
            hi = value.astype(jnp.bfloat16).astype(jnp.float32)
            left[:, where] = jnp.concatenate([hi, value - hi], axis=0).astype(jnp.bfloat16)
    acc = lax.dot_general(left[...], table[...], (((1,), (1,)), ((), ())), preferred_element_type=jnp.float32)
    sums = (acc[0:8, 0:128] + acc[0:8, 128:256]) + (acc[8:16, 0:128] + acc[8:16, 128:256])
    shape = (128, 128)
    column = lax.broadcasted_iota(jnp.int32, shape, 1)
    pick = jnp.where(lax.broadcasted_iota(jnp.int32, shape, 0) == 2 * (column - 64), 1.0, 0.0).astype(jnp.float32)
    even = jnp.dot(sums, pick, precision=lax.Precision.HIGHEST, preferred_element_type=jnp.float32)
    out_ref[0:8] = jnp.round((128.0 + 0.5 * even) * NORM_STEPS)
    out_ref[8:16] = jnp.zeros((8, 128), jnp.float32)


def arrange_kernel(scalars, d0, d1, d2, d3, out_ref, rows_ref, rows):
    g = scalars[0]
    for slot, ref in enumerate((d0, d1, d2, d3)):
        rows[pl.ds(pl.multiple_of(lax.rem(g + slot, 4) * 64, 64), 64), :] = ref[...]
    rows_ref[...] = rows[...]
    for half in range(2):
        turned = rows[:, half * 512 : half * 512 + 512].astype(jnp.float32).T.astype(jnp.bfloat16)
        out_ref[:, half * 16 : half * 16 + 16, :] = turned.reshape(32, 16, 256)


def partial_kernel(scalars, data_ref, table_in, factor_ref, keep_ref, give_ref, acc, left0, left1, table_ref, sems):
    dims = (((1,), (1,)), ((), ()))

    def fetch(b):
        return pltpu.make_async_copy(table_in.at[b], table_ref.at[b], sems.at[b])

    for b in range(16):
        fetch(b).start()

    def generate(b, left):
        for part in range(4):
            q = b * 2 + part // 2
            cols = slice(part % 2 * 128, part % 2 * 128 + 128)
            data = data_ref[q, :, cols].astype(jnp.float32)
            lanes = slice(part * 128, part * 128 + 128)
            lanes_s = slice(512 + part * 128, 512 + part * 128 + 128)
            for jh in range(4):
                rows = slice(jh * 32, jh * 32 + 32)
                rows_lo = slice(128 + jh * 32, 128 + jh * 32 + 32)
                left[rows, lanes], left[rows_lo, lanes] = split(data * factor_ref[q, jh : jh + 1, cols])
                left[rows, lanes_s], left[rows_lo, lanes_s] = split(data * factor_ref[q, 4 + jh : 5 + jh, cols])

    def multiply(b, left):
        acc[...] += lax.dot_general(left[...], table_ref[b], dims, preferred_element_type=jnp.float32)

    acc[...] = jnp.zeros_like(acc)
    generate(0, left0)

    def block(i, carry):
        generate(2 * i + 1, left1)
        multiply(2 * i, left0)
        generate(2 * i + 2, left0)
        multiply(2 * i + 1, left1)
        return carry

    for first, last in ((0, 1), (1, 2), (2, 4), (4, 6), (6, 8)):
        for b in range(2 * first, 2 * last):
            fetch(b).wait()
        lax.fori_loop(first, min(last, 7), block, 0)
    generate(15, left1)
    multiply(14, left0)
    multiply(15, left1)
    first = scalars[0] == 0
    for jh in range(4):
        lanes = slice(jh * 128, jh * 128 + 128)
        row = slice(jh * 32, jh * 32 + 32)
        row_lo = slice(128 + jh * 32, 128 + jh * 32 + 32)
        both = (acc[row, 0:128] + acc[row, 128:256]) + (acc[row_lo, 0:128] + acc[row_lo, 128:256])
        keep_ref[:, lanes] = jnp.where(first, both[0:16], both[16:32])
        give_ref[:, lanes] = jnp.where(first, both[16:32], both[0:16])


def code_kernel(keep_ref, other_ref, norm_ref, out_ref):
    piece = keep_ref[...] + other_ref[...]
    most = jnp.max(jnp.abs(piece), axis=1, keepdims=True)
    power = jnp.ceil(jnp.log2(jnp.maximum(most, 2.0**-60)))
    mantissa = jnp.ceil(most * jnp.exp2(-power) * 16384.0) + 1.0
    unit = mantissa * jnp.exp2(power) * (1.0 / (16384.0 * 32767.0))
    code = jnp.round(piece * (1.0 / unit))
    lane = lax.broadcasted_iota(jnp.int32, (16, 128), 1)
    scale = jnp.where(lane == 0, mantissa, jnp.where(lane == 1, power, norm_ref[...]))
    whole = jnp.concatenate([code, scale], axis=1).astype(jnp.int32).astype(jnp.int16)
    for q in range(32):
        out_ref[q] = whole


def decode(ref):
    scale = ref[:, :, 512:640].astype(jnp.int32).astype(jnp.float32)
    tail = scale.reshape(512, 128)
    unit = tail[:, 0:1] * jnp.exp2(tail[:, 1:2]) * (1.0 / (16384.0 * 32767.0))
    codes = ref[:, :, 0:512].astype(jnp.int32).astype(jnp.float32).reshape(512, 512)
    return codes * unit, jnp.sum(scale, axis=0)


def product(half, ref, data):
    p, tail = decode(ref)
    high, low = split(p * (1.0 / SNAP))
    left = data[:, pl.ds(pl.multiple_of(half * 512, 512), 512)]
    total = jnp.dot(left, high, preferred_element_type=jnp.float32) + jnp.dot(left, low, preferred_element_type=jnp.float32)
    return total, jnp.sum(p * p, axis=0, keepdims=True), tail


def own_kernel(scalars, half_ref, data, out_ref, forms_ref, tail_ref):
    out_ref[...], forms_ref[...], tail_ref[...] = product(scalars[0], half_ref, data)


def final_kernel(scalars, half_ref, data, own_ref, forms_ref, tail_ref, gamma_ref, noise_ref, out_ref, gamma_out):
    total, forms, tails = product(1 - scalars[0], half_ref, data)
    out_ref[...] = own_ref[...] + total
    forms = forms + forms_ref[...]
    tails = tails + tail_ref[...]
    rolled = pltpu.roll(tails, 64, 1)
    below = lax.broadcasted_iota(jnp.int32, (1, 128), 1) < 64
    pieces = [jnp.where(below, rolled[2 * t : 2 * t + 1], tails[2 * t + 1 : 2 * t + 2]) for t in range(4)]
    norms = jnp.concatenate(pieces, axis=1) * (1.0 / NORM_STEPS)
    gamma = gamma_ref[...]
    gamma_out[...] = gamma * (forms * (1.0 / SNAP)) / (norms * (gamma + noise_ref[0]))


VMEM = pl.BlockSpec(memory_space=pltpu.VMEM)
SMEM = pl.BlockSpec(memory_space=pltpu.SMEM)
HBM = pl.BlockSpec(memory_space=pltpu.HBM)


def call(kernel, name, mib, outs, in_specs, scratch=(), out_specs=None):
    return pl.pallas_call(
        kernel,
        out_shape=tuple(jax.ShapeDtypeStruct(*o) for o in outs),
        in_specs=in_specs,
        out_specs=out_specs or (VMEM,) * len(outs),
        scratch_shapes=scratch,
        compiler_params=pltpu.CompilerParams(vmem_limit_bytes=mib * 2**20),
        name=name,
    )


def on_device(snapshots, jitter_code, slab_start, gamma, noise_var):
    core = lax.axis_index("core").astype(jnp.int32)
    g = lax.axis_index("grid").astype(jnp.int32)
    swap = [(0, 1), (1, 0)]
    f32 = jnp.float32
    slots = [lax.ppermute(snapshots, "grid", [((i + s) % 4, i) for i in range(4)]) for s in (1, 2, 3)]
    bf16 = jnp.bfloat16
    q = lax.axis_index(PLANE).astype(jnp.int32)
    codes = jitter_code.reshape(128, 128)
    dma = pltpu.SemaphoreType.DMA((16,))
    table, factor, own = call(
        table_kernel,
        "table",
        48,
        [((16, 256, 1024), bf16), ((32, 8, 256), f32), ((64, 1024), bf16)],
        [SMEM, VMEM, VMEM],
        [pltpu.VMEM((16, 256, 1024), bf16), dma],
        (HBM, VMEM, VMEM),
    )(jnp.stack([core, slab_start[0]]), codes, snapshots)
    place = jnp.stack([core, slab_start[0], q])
    table, own, slots, codes, place = lax.optimization_barrier((table, own, slots, codes, place))
    turned, rows = call(
        arrange_kernel,
        "arrange",
        8,
        [((32, 32, 256), bf16), ((256, 1024), bf16)],
        [SMEM] + [VMEM] * 4,
        [pltpu.VMEM((256, 1024), bf16)],
    )(g[None], own, *slots)
    mixed = lax.all_to_all(turned, PLANE, 0, 0, tiled=True)
    keep, give = call(
        partial_kernel,
        "partial",
        48,
        [((16, 512), f32), ((16, 512), f32)],
        [SMEM, VMEM, HBM, VMEM],
        [pltpu.VMEM((256, 256), f32)]
        + [pltpu.VMEM((256, 1024), bf16)] * 2
        + [pltpu.VMEM((16, 256, 1024), bf16), dma],
    )(core[None], mixed, table, factor)
    keep, give, codes, place = lax.optimization_barrier((keep, give, codes, place))
    other = lax.ppermute(give, "core", swap)
    (norm,) = call(
        norm_kernel,
        "norm",
        8,
        [((16, 128), f32)],
        [SMEM, VMEM],
        [pltpu.VMEM((256, 512), bf16), pltpu.VMEM((16, 512), bf16)],
    )(place, codes)
    (coded,) = call(code_kernel, "code", 8, [((32, 16, 640), jnp.int16)], [VMEM] * 3)(
        keep, other, norm
    )
    half = lax.all_to_all(coded, PLANE, 0, 0, tiled=True)
    half_other = lax.ppermute(half, "core", swap)
    own_part = call(
        own_kernel,
        "own",
        12,
        [((256, 512), f32), ((1, 512), f32), ((16, 128), f32)],
        [SMEM, VMEM, VMEM],
    )(core[None], half, rows)
    steered, gamma_new = call(
        final_kernel,
        "final",
        12,
        [((256, 512), f32), ((1, 512), f32)],
        [SMEM] + [VMEM] * 6 + [SMEM],
    )(core[None], half_other, rows, *own_part, gamma.reshape(1, 512), noise_var)
    return steered, gamma_new.reshape(512)


def solution(mesh):
    fine = Mesh(mesh.devices.reshape(4, 2, 4, 2, 4), ("x", "zl", "y", "core", "grid"))
    sensors = ("x", "zl", "y", "core")
    in_specs = (P((*sensors, "grid"), None), P(), P("grid"), P("grid"), P())
    out_specs = (P(sensors, "grid"), P("grid"))
    return jax.shard_map(on_device, mesh=fine, in_specs=in_specs, out_specs=out_specs, check_vma=False)
```

```python
import jax
import jax.numpy as jnp
import numpy as np
from jax import lax
from jax.experimental import pallas as pl
from jax.experimental.pallas import tpu as pltpu
from jax.sharding import Mesh, PartitionSpec as P

SNAP = 1024
PLANE = ("x", "zl", "y")
NORM_STEPS = 127.9


def fit_sine():
    v = np.cos(np.linspace(0.0, np.pi, 4001)) * 0.25
    basis = np.stack([v ** (2 * i + 1) for i in range(6)], axis=1)
    return tuple(float(c) for c in np.linalg.lstsq(basis, np.sin(2 * np.pi * v), rcond=None)[0])


COEF = fit_sine()


def sine_poly(v):
    w = v * v
    total = jnp.float32(COEF[5])
    for c in COEF[4::-1]:
        total = total * w + jnp.float32(c)
    return total * v


def cos_sin(angle):
    turns = (angle << 10).astype(jnp.float32) * jnp.float32(2.0**-32)
    size = jnp.abs(turns)
    v = size - 0.25
    cosine = -sine_poly(v)
    sine = sine_poly(0.25 - jnp.abs(v))
    return cosine, jnp.where(turns < 0, -sine, sine)


def split(x):
    high = x.astype(jnp.bfloat16)
    return high, (x - high.astype(jnp.float32)).astype(jnp.bfloat16)


def angles(scalars, start_row):
    sub = lax.broadcasted_iota(jnp.int32, (8, 128), 0)
    lane = lax.broadcasted_iota(jnp.int32, (8, 128), 1)
    start = jnp.where(sub == 0, start_row, jnp.where(sub == 1, 1024, 2048))
    return sub, lane + scalars[0] * 256, start, jnp.where(sub == 0, 1 << 15, 0)


def fill_table(pos, constants, table, lanes, lanes_s):
    sub, _, start, keep = constants
    c, s = cos_sin(pos * (sub * 128))
    cc, sc = cos_sin(pos * (sub * 16384))
    ca, sa = cos_sin(pos * start - (pos & 127) * keep)
    c8, s8, c16, s16 = ca[1:2], sa[1:2], ca[2:3], sa[2:3]
    c, s = jnp.concatenate([c, c * c8 - s * s8], axis=0), jnp.concatenate([s, s * c8 + c * s8], axis=0)
    for step in range(8):
        rows = slice(step * 16, step * 16 + 16)
        rows_lo = slice(128 + step * 16, 128 + step * 16 + 16)
        table[rows, lanes], table[rows_lo, lanes] = split(c)
        table[rows, lanes_s], table[rows_lo, lanes_s] = split(s)
        if step < 7:
            c, s = c * c16 - s * s16, s * c16 + c * s16
    return cc, sc, ca[0:1], sa[0:1]


def table_kernel(scalars, jit_ref, rows_ref, table_out, head_ref, factor_ref, own_ref, table_ref, sems):
    own_ref[...] = rows_ref[...]
    constants = angles(scalars, scalars[1])

    def store(b):
        return pltpu.make_async_copy(table_ref.at[b], table_out.at[b], sems.at[b])

    def block(b, carry):
        for part in range(4):
            q = b * 2 + part // 2
            half = part % 2
            cols = slice(half * 128, half * 128 + 128)
            pos = (q * 512 + constants[1] + half * 128) * 64 + jit_ref[pl.ds(q * 4 + scalars[0] * 2 + half, 1), :] + 32
            lanes = slice(part * 128, part * 128 + 128)
            lanes_s = slice(512 + part * 128, 512 + part * 128 + 128)
            cc, sc, ra, rs = fill_table(pos, constants, table_ref.at[b], lanes, lanes_s)
            fc, fs = ra * cc - rs * sc, -(rs * cc + ra * sc)
            factor_ref[q, :, cols] = jnp.concatenate([fc[0:4], fs[0:4]], axis=0)
        store(b).start()
        return carry

    lax.fori_loop(0, 16, block, 0)
    head_ref[...] = table_ref[0:2]
    for b in range(16):
        store(b).wait()


def norm_kernel(scalars, jit_ref, out_ref, table, left):
    constants = angles(scalars, scalars[1])
    q = scalars[2]
    for part in range(2):
        pos = (q * 512 + constants[1] + part * 128) * 64 + jit_ref[pl.ds(q * 4 + scalars[0] * 2 + part, 1), :] + 32
        lanes = slice(part * 128, part * 128 + 128)
        lanes_s = slice(256 + part * 128, 256 + part * 128 + 128)
        cc, sc, ra, rs = fill_table(pos, constants, table, lanes, lanes_s)
        r2, s2 = 2.0 * ra * ra - 1.0, 2.0 * ra * rs
        for value, where in ((r2 * cc - s2 * sc, lanes), (-(s2 * cc + r2 * sc), lanes_s)):
            hi = value.astype(jnp.bfloat16).astype(jnp.float32)
            left[:, where] = jnp.concatenate([hi, value - hi], axis=0).astype(jnp.bfloat16)
    acc = lax.dot_general(left[...], table[...], (((1,), (1,)), ((), ())), preferred_element_type=jnp.float32)
    sums = (acc[0:8, 0:128] + acc[0:8, 128:256]) + (acc[8:16, 0:128] + acc[8:16, 128:256])
    shape = (128, 128)
    column = lax.broadcasted_iota(jnp.int32, shape, 1)
    pick = jnp.where(lax.broadcasted_iota(jnp.int32, shape, 0) == 2 * (column - 64), 1.0, 0.0).astype(jnp.float32)
    even = jnp.dot(sums, pick, precision=lax.Precision.HIGHEST, preferred_element_type=jnp.float32)
    out_ref[0:8] = jnp.round((128.0 + 0.5 * even) * NORM_STEPS)
    out_ref[8:16] = jnp.zeros((8, 128), jnp.float32)


def arrange_kernel(scalars, d0, d1, d2, d3, out_ref, rows_ref, rows):
    g = scalars[0]
    for slot, ref in enumerate((d0, d1, d2, d3)):
        rows[pl.ds(pl.multiple_of(lax.rem(g + slot, 4) * 64, 64), 64), :] = ref[...]
    rows_ref[...] = rows[...]
    for half in range(2):
        turned = rows[:, half * 512 : half * 512 + 512].astype(jnp.float32).T.astype(jnp.bfloat16)
        out_ref[:, half * 16 : half * 16 + 16, :] = turned.reshape(32, 16, 256)


def partial_kernel(scalars, data_ref, table_in, head_ref, factor_ref, keep_ref, give_ref, acc, left0, left1, table_ref, sems):
    dims = (((1,), (1,)), ((), ()))

    def fetch(b):
        return pltpu.make_async_copy(table_in.at[b], table_ref.at[b], sems.at[b])

    for b in range(2, 16):
        fetch(b).start()

    def generate(b, left):
        for part in range(4):
            q = b * 2 + part // 2
            cols = slice(part % 2 * 128, part % 2 * 128 + 128)
            data = data_ref[q, :, cols].astype(jnp.float32)
            lanes = slice(part * 128, part * 128 + 128)
            lanes_s = slice(512 + part * 128, 512 + part * 128 + 128)
            for jh in range(4):
                rows = slice(jh * 32, jh * 32 + 32)
                rows_lo = slice(128 + jh * 32, 128 + jh * 32 + 32)
                left[rows, lanes], left[rows_lo, lanes] = split(data * factor_ref[q, jh : jh + 1, cols])
                left[rows, lanes_s], left[rows_lo, lanes_s] = split(data * factor_ref[q, 4 + jh : 5 + jh, cols])

    def multiply(b, left, tables=table_ref):
        acc[...] += lax.dot_general(left[...], tables[b], dims, preferred_element_type=jnp.float32)

    acc[...] = jnp.zeros_like(acc)
    generate(0, left0)

    def block(i, carry):
        generate(2 * i + 1, left1)
        multiply(2 * i, left0)
        generate(2 * i + 2, left0)
        multiply(2 * i + 1, left1)
        return carry

    generate(1, left1)
    multiply(0, left0, head_ref)
    generate(2, left0)
    multiply(1, left1, head_ref)
    for first, last in ((1, 2), (2, 4), (4, 6), (6, 8)):
        for b in range(2 * first, 2 * last):
            fetch(b).wait()
        lax.fori_loop(first, min(last, 7), block, 0)
    generate(15, left1)
    multiply(14, left0)
    multiply(15, left1)
    first = scalars[0] == 0
    for jh in range(4):
        lanes = slice(jh * 128, jh * 128 + 128)
        row = slice(jh * 32, jh * 32 + 32)
        row_lo = slice(128 + jh * 32, 128 + jh * 32 + 32)
        both = (acc[row, 0:128] + acc[row, 128:256]) + (acc[row_lo, 0:128] + acc[row_lo, 128:256])
        keep_ref[:, lanes] = jnp.where(first, both[0:16], both[16:32])
        give_ref[:, lanes] = jnp.where(first, both[16:32], both[0:16])


def code_kernel(keep_ref, other_ref, norm_ref, out_ref):
    piece = keep_ref[...] + other_ref[...]
    most = jnp.max(jnp.abs(piece), axis=1, keepdims=True)
    power = jnp.ceil(jnp.log2(jnp.maximum(most, 2.0**-60)))
    mantissa = jnp.ceil(most * jnp.exp2(-power) * 16384.0) + 1.0
    unit = mantissa * jnp.exp2(power) * (1.0 / (16384.0 * 32767.0))
    code = jnp.round(piece * (1.0 / unit))
    lane = lax.broadcasted_iota(jnp.int32, (16, 128), 1)
    scale = jnp.where(lane == 0, mantissa, jnp.where(lane == 1, power, norm_ref[...]))
    whole = jnp.concatenate([code, scale], axis=1).astype(jnp.int32).astype(jnp.int16)
    for q in range(32):
        out_ref[q] = whole


def decode(ref):
    scale = ref[:, :, 512:640].astype(jnp.int32).astype(jnp.float32)
    tail = scale.reshape(512, 128)
    unit = tail[:, 0:1] * jnp.exp2(tail[:, 1:2]) * (1.0 / (16384.0 * 32767.0))
    codes = ref[:, :, 0:512].astype(jnp.int32).astype(jnp.float32).reshape(512, 512)
    return codes * unit, jnp.sum(scale, axis=0)


def product(half, ref, data):
    p, tail = decode(ref)
    high, low = split(p * (1.0 / SNAP))
    left = data[:, pl.ds(pl.multiple_of(half * 512, 512), 512)]
    total = jnp.dot(left, high, preferred_element_type=jnp.float32) + jnp.dot(left, low, preferred_element_type=jnp.float32)
    return total, jnp.sum(p * p, axis=0, keepdims=True), tail


def own_kernel(scalars, half_ref, data, out_ref, forms_ref, tail_ref):
    out_ref[...], forms_ref[...], tail_ref[...] = product(scalars[0], half_ref, data)


def final_kernel(scalars, half_ref, data, own_ref, forms_ref, tail_ref, gamma_ref, noise_ref, out_ref, gamma_out):
    total, forms, tails = product(1 - scalars[0], half_ref, data)
    out_ref[...] = own_ref[...] + total
    forms = forms + forms_ref[...]
    tails = tails + tail_ref[...]
    rolled = pltpu.roll(tails, 64, 1)
    below = lax.broadcasted_iota(jnp.int32, (1, 128), 1) < 64
    pieces = [jnp.where(below, rolled[2 * t : 2 * t + 1], tails[2 * t + 1 : 2 * t + 2]) for t in range(4)]
    norms = jnp.concatenate(pieces, axis=1) * (1.0 / NORM_STEPS)
    gamma = gamma_ref[...]
    gamma_out[...] = gamma * (forms * (1.0 / SNAP)) / (norms * (gamma + noise_ref[0]))


VMEM = pl.BlockSpec(memory_space=pltpu.VMEM)
SMEM = pl.BlockSpec(memory_space=pltpu.SMEM)
HBM = pl.BlockSpec(memory_space=pltpu.HBM)


def call(kernel, name, mib, outs, in_specs, scratch=(), out_specs=None):
    return pl.pallas_call(
        kernel,
        out_shape=tuple(jax.ShapeDtypeStruct(*o) for o in outs),
        in_specs=in_specs,
        out_specs=out_specs or (VMEM,) * len(outs),
        scratch_shapes=scratch,
        compiler_params=pltpu.CompilerParams(vmem_limit_bytes=mib * 2**20),
        name=name,
    )


def on_device(snapshots, jitter_code, slab_start, gamma, noise_var):
    core = lax.axis_index("core").astype(jnp.int32)
    g = lax.axis_index("grid").astype(jnp.int32)
    swap = [(0, 1), (1, 0)]
    f32 = jnp.float32
    slots = [lax.ppermute(snapshots, "grid", [((i + s) % 4, i) for i in range(4)]) for s in (1, 2, 3)]
    bf16 = jnp.bfloat16
    q = lax.axis_index(PLANE).astype(jnp.int32)
    codes = jitter_code.reshape(128, 128)
    dma = pltpu.SemaphoreType.DMA((16,))
    table, head, factor, own = call(
        table_kernel,
        "table",
        48,
        [((16, 256, 1024), bf16), ((2, 256, 1024), bf16), ((32, 8, 256), f32), ((64, 1024), bf16)],
        [SMEM, VMEM, VMEM],
        [pltpu.VMEM((16, 256, 1024), bf16), dma],
        (HBM, VMEM, VMEM, VMEM),
    )(jnp.stack([core, slab_start[0]]), codes, snapshots)
    place = jnp.stack([core, slab_start[0], q])
    table, own, slots, codes, place = lax.optimization_barrier((table, own, slots, codes, place))
    turned, rows = call(
        arrange_kernel,
        "arrange",
        8,
        [((32, 32, 256), bf16), ((256, 1024), bf16)],
        [SMEM] + [VMEM] * 4,
        [pltpu.VMEM((256, 1024), bf16)],
    )(g[None], own, *slots)
    mixed = lax.all_to_all(turned, PLANE, 0, 0, tiled=True)
    keep, give = call(
        partial_kernel,
        "partial",
        48,
        [((16, 512), f32), ((16, 512), f32)],
        [SMEM, VMEM, HBM, VMEM, VMEM],
        [pltpu.VMEM((256, 256), f32)]
        + [pltpu.VMEM((256, 1024), bf16)] * 2
        + [pltpu.VMEM((16, 256, 1024), bf16), dma],
    )(core[None], mixed, table, head, factor)
    keep, give, codes, place = lax.optimization_barrier((keep, give, codes, place))
    other = lax.ppermute(give, "core", swap)
    (norm,) = call(
        norm_kernel,
        "norm",
        8,
        [((16, 128), f32)],
        [SMEM, VMEM],
        [pltpu.VMEM((256, 512), bf16), pltpu.VMEM((16, 512), bf16)],
    )(place, codes)
    (coded,) = call(code_kernel, "code", 8, [((32, 16, 640), jnp.int16)], [VMEM] * 3)(
        keep, other, norm
    )
    half = lax.all_to_all(coded, PLANE, 0, 0, tiled=True)
    half_other = lax.ppermute(half, "core", swap)
    own_part = call(
        own_kernel,
        "own",
        12,
        [((256, 512), f32), ((1, 512), f32), ((16, 128), f32)],
        [SMEM, VMEM, VMEM],
    )(core[None], half, rows)
    steered, gamma_new = call(
        final_kernel,
        "final",
        12,
        [((256, 512), f32), ((1, 512), f32)],
        [SMEM] + [VMEM] * 6 + [SMEM],
    )(core[None], half_other, rows, *own_part, gamma.reshape(1, 512), noise_var)
    return steered, gamma_new.reshape(512)


def solution(mesh):
    fine = Mesh(mesh.devices.reshape(4, 2, 4, 2, 4), ("x", "zl", "y", "core", "grid"))
    sensors = ("x", "zl", "y", "core")
    in_specs = (P((*sensors, "grid"), None), P(), P("grid"), P("grid"), P())
    out_specs = (P(sensors, "grid"), P("grid"))
    return jax.shard_map(on_device, mesh=fine, in_specs=in_specs, out_specs=out_specs, check_vma=False)
```

```python
import jax
import jax.numpy as jnp
import numpy as np
from jax import lax
from jax.experimental import pallas as pl
from jax.experimental.pallas import tpu as pltpu
from jax.sharding import Mesh, PartitionSpec as P

SNAP = 1024
PLANE = ("x", "zl", "y")
NORM_STEPS = 127.9


def fit_sine():
    v = np.cos(np.linspace(0.0, np.pi, 4001)) * 0.25
    basis = np.stack([v ** (2 * i + 1) for i in range(6)], axis=1)
    return tuple(float(c) for c in np.linalg.lstsq(basis, np.sin(2 * np.pi * v), rcond=None)[0])


COEF = fit_sine()


def sine_poly(v):
    w = v * v
    total = jnp.float32(COEF[5])
    for c in COEF[4::-1]:
        total = total * w + jnp.float32(c)
    return total * v


def cos_sin(angle):
    turns = (angle << 10).astype(jnp.float32) * jnp.float32(2.0**-32)
    size = jnp.abs(turns)
    v = size - 0.25
    cosine = -sine_poly(v)
    sine = sine_poly(0.25 - jnp.abs(v))
    return cosine, jnp.where(turns < 0, -sine, sine)


def split(x):
    high = x.astype(jnp.bfloat16)
    return high, (x - high.astype(jnp.float32)).astype(jnp.bfloat16)


def angles(scalars, start_row):
    sub = lax.broadcasted_iota(jnp.int32, (8, 128), 0)
    lane = lax.broadcasted_iota(jnp.int32, (8, 128), 1)
    start = jnp.where(sub == 0, start_row, jnp.where(sub == 1, 1024, 2048))
    return sub, lane + scalars[0] * 256, start, jnp.where(sub == 0, 1 << 15, 0)


def fill_table(pos, constants, table, lanes, lanes_s):
    sub, _, start, keep = constants
    c, s = cos_sin(pos * (sub * 128))
    cc, sc = cos_sin(pos * (sub * 16384))
    ca, sa = cos_sin(pos * start - (pos & 127) * keep)
    c8, s8, c16, s16 = ca[1:2], sa[1:2], ca[2:3], sa[2:3]
    c, s = jnp.concatenate([c, c * c8 - s * s8], axis=0), jnp.concatenate([s, s * c8 + c * s8], axis=0)
    for step in range(8):
        rows = slice(step * 16, step * 16 + 16)
        rows_lo = slice(128 + step * 16, 128 + step * 16 + 16)
        table[rows, lanes], table[rows_lo, lanes] = split(c)
        table[rows, lanes_s], table[rows_lo, lanes_s] = split(s)
        if step < 7:
            c, s = c * c16 - s * s16, s * c16 + c * s16
    return cc, sc, ca[0:1], sa[0:1]


def table_kernel(scalars, jit_ref, rows_ref, table_out, head_ref, factor_ref, own_ref, table_ref, sems):
    own_ref[...] = rows_ref[...]
    constants = angles(scalars, scalars[1])

    def store(b):
        return pltpu.make_async_copy(table_ref.at[b], table_out.at[b], sems.at[b])

    def block(b, carry):
        for part in range(4):
            q = b * 2 + part // 2
            half = part % 2
            cols = slice(half * 128, half * 128 + 128)
            pos = (q * 512 + constants[1] + half * 128) * 64 + jit_ref[pl.ds(q * 4 + scalars[0] * 2 + half, 1), :] + 32
            lanes = slice(part * 128, part * 128 + 128)
            lanes_s = slice(512 + part * 128, 512 + part * 128 + 128)
            cc, sc, ra, rs = fill_table(pos, constants, table_ref.at[b], lanes, lanes_s)
            fc, fs = ra * cc - rs * sc, -(rs * cc + ra * sc)
            factor_ref[q, :, cols] = jnp.concatenate([fc[0:4], fs[0:4]], axis=0)
        store(b).start()
        return carry

    lax.fori_loop(0, 16, block, 0)
    head_ref[...] = table_ref[0:2]
    for b in range(16):
        store(b).wait()


def norm_kernel(scalars, jit_ref, out_ref, table, left):
    constants = angles(scalars, scalars[1])
    q = scalars[2]
    for part in range(2):
        pos = (q * 512 + constants[1] + part * 128) * 64 + jit_ref[pl.ds(q * 4 + scalars[0] * 2 + part, 1), :] + 32
        lanes = slice(part * 128, part * 128 + 128)
        lanes_s = slice(256 + part * 128, 256 + part * 128 + 128)
        cc, sc, ra, rs = fill_table(pos, constants, table, lanes, lanes_s)
        r2, s2 = 2.0 * ra * ra - 1.0, 2.0 * ra * rs
        for value, where in ((r2 * cc - s2 * sc, lanes), (-(s2 * cc + r2 * sc), lanes_s)):
            hi = value.astype(jnp.bfloat16).astype(jnp.float32)
            left[:, where] = jnp.concatenate([hi, value - hi], axis=0).astype(jnp.bfloat16)
    acc = lax.dot_general(left[...], table[...], (((1,), (1,)), ((), ())), preferred_element_type=jnp.float32)
    sums = (acc[0:8, 0:128] + acc[0:8, 128:256]) + (acc[8:16, 0:128] + acc[8:16, 128:256])
    shape = (128, 128)
    column = lax.broadcasted_iota(jnp.int32, shape, 1)
    pick = jnp.where(lax.broadcasted_iota(jnp.int32, shape, 0) == 2 * (column - 64), 1.0, 0.0).astype(jnp.float32)
    even = jnp.dot(sums, pick, precision=lax.Precision.HIGHEST, preferred_element_type=jnp.float32)
    out_ref[0:8] = jnp.round((128.0 + 0.5 * even) * NORM_STEPS)
    out_ref[8:16] = jnp.zeros((8, 128), jnp.float32)


def arrange_kernel(scalars, d0, d2, d1, d3, out_ref, rows_ref, rows):
    g = scalars[0]
    for slot, ref in enumerate((d0, d1, d2, d3)):
        rows[pl.ds(pl.multiple_of(lax.rem(g + slot, 4) * 64, 64), 64), :] = ref[...]
    rows_ref[...] = rows[...]
    for half in range(2):
        turned = rows[:, half * 512 : half * 512 + 512].astype(jnp.float32).T.astype(jnp.bfloat16)
        out_ref[:, half * 16 : half * 16 + 16, :] = turned.reshape(32, 16, 256)


def partial_kernel(scalars, data_ref, table_in, head_ref, factor_ref, keep_ref, give_ref, acc, left0, left1, table_ref, sems):
    dims = (((1,), (1,)), ((), ()))

    def fetch(b):
        return pltpu.make_async_copy(table_in.at[b], table_ref.at[b], sems.at[b])

    for b in range(2, 16):
        fetch(b).start()

    def generate(b, left):
        for part in range(4):
            q = b * 2 + part // 2
            cols = slice(part % 2 * 128, part % 2 * 128 + 128)
            data = data_ref[q, :, cols].astype(jnp.float32)
            lanes = slice(part * 128, part * 128 + 128)
            lanes_s = slice(512 + part * 128, 512 + part * 128 + 128)
            for jh in range(4):
                rows = slice(jh * 32, jh * 32 + 32)
                rows_lo = slice(128 + jh * 32, 128 + jh * 32 + 32)
                left[rows, lanes], left[rows_lo, lanes] = split(data * factor_ref[q, jh : jh + 1, cols])
                left[rows, lanes_s], left[rows_lo, lanes_s] = split(data * factor_ref[q, 4 + jh : 5 + jh, cols])

    def multiply(b, left, tables=table_ref):
        acc[...] += lax.dot_general(left[...], tables[b], dims, preferred_element_type=jnp.float32)

    acc[...] = jnp.zeros_like(acc)
    generate(0, left0)

    def block(i, carry):
        generate(2 * i + 1, left1)
        multiply(2 * i, left0)
        generate(2 * i + 2, left0)
        multiply(2 * i + 1, left1)
        return carry

    generate(1, left1)
    multiply(0, left0, head_ref)
    generate(2, left0)
    multiply(1, left1, head_ref)
    for first, last in ((1, 2), (2, 4), (4, 6), (6, 8)):
        for b in range(2 * first, 2 * last):
            fetch(b).wait()
        lax.fori_loop(first, min(last, 7), block, 0)
    generate(15, left1)
    multiply(14, left0)
    multiply(15, left1)
    first = scalars[0] == 0
    for jh in range(4):
        lanes = slice(jh * 128, jh * 128 + 128)
        row = slice(jh * 32, jh * 32 + 32)
        row_lo = slice(128 + jh * 32, 128 + jh * 32 + 32)
        both = (acc[row, 0:128] + acc[row, 128:256]) + (acc[row_lo, 0:128] + acc[row_lo, 128:256])
        keep_ref[:, lanes] = jnp.where(first, both[0:16], both[16:32])
        give_ref[:, lanes] = jnp.where(first, both[16:32], both[0:16])


def code_kernel(keep_ref, other_ref, norm_ref, out_ref):
    piece = keep_ref[...] + other_ref[...]
    most = jnp.max(jnp.abs(piece), axis=1, keepdims=True)
    power = jnp.ceil(jnp.log2(jnp.maximum(most, 2.0**-60)))
    mantissa = jnp.ceil(most * jnp.exp2(-power) * 16384.0) + 1.0
    unit = mantissa * jnp.exp2(power) * (1.0 / (16384.0 * 32767.0))
    code = jnp.round(piece * (1.0 / unit))
    lane = lax.broadcasted_iota(jnp.int32, (16, 128), 1)
    scale = jnp.where(lane == 0, mantissa, jnp.where(lane == 1, power, norm_ref[...]))
    whole = jnp.concatenate([code, scale], axis=1).astype(jnp.int32).astype(jnp.int16)
    for q in range(32):
        out_ref[q] = whole


def decode(ref):
    scale = ref[:, :, 512:640].astype(jnp.int32).astype(jnp.float32)
    tail = scale.reshape(512, 128)
    unit = tail[:, 0:1] * jnp.exp2(tail[:, 1:2]) * (1.0 / (16384.0 * 32767.0))
    codes = ref[:, :, 0:512].astype(jnp.int32).astype(jnp.float32).reshape(512, 512)
    return codes * unit, jnp.sum(scale, axis=0)


def product(half, ref, data):
    p, tail = decode(ref)
    high, low = split(p * (1.0 / SNAP))
    left = data[:, pl.ds(pl.multiple_of(half * 512, 512), 512)]
    total = jnp.dot(left, high, preferred_element_type=jnp.float32) + jnp.dot(left, low, preferred_element_type=jnp.float32)
    return total, jnp.sum(p * p, axis=0, keepdims=True), tail


def own_kernel(scalars, half_ref, data, out_ref, forms_ref, tail_ref):
    out_ref[...], forms_ref[...], tail_ref[...] = product(scalars[0], half_ref, data)


def final_kernel(scalars, half_ref, data, own_ref, forms_ref, tail_ref, gamma_ref, noise_ref, out_ref, gamma_out):
    total, forms, tails = product(1 - scalars[0], half_ref, data)
    out_ref[...] = own_ref[...] + total
    forms = forms + forms_ref[...]
    tails = tails + tail_ref[...]
    rolled = pltpu.roll(tails, 64, 1)
    below = lax.broadcasted_iota(jnp.int32, (1, 128), 1) < 64
    pieces = [jnp.where(below, rolled[2 * t : 2 * t + 1], tails[2 * t + 1 : 2 * t + 2]) for t in range(4)]
    norms = jnp.concatenate(pieces, axis=1) * (1.0 / NORM_STEPS)
    gamma = gamma_ref[...]
    gamma_out[...] = gamma * (forms * (1.0 / SNAP)) / (norms * (gamma + noise_ref[0]))


VMEM = pl.BlockSpec(memory_space=pltpu.VMEM)
SMEM = pl.BlockSpec(memory_space=pltpu.SMEM)
HBM = pl.BlockSpec(memory_space=pltpu.HBM)


def call(kernel, name, mib, outs, in_specs, scratch=(), out_specs=None):
    return pl.pallas_call(
        kernel,
        out_shape=tuple(jax.ShapeDtypeStruct(*o) for o in outs),
        in_specs=in_specs,
        out_specs=out_specs or (VMEM,) * len(outs),
        scratch_shapes=scratch,
        compiler_params=pltpu.CompilerParams(vmem_limit_bytes=mib * 2**20),
        name=name,
    )


def on_device(snapshots, jitter_code, slab_start, gamma, noise_var):
    core = lax.axis_index("core").astype(jnp.int32)
    g = lax.axis_index("grid").astype(jnp.int32)
    swap = [(0, 1), (1, 0)]
    f32 = jnp.float32
    slots = [lax.ppermute(snapshots, "grid", [((i + s) % 4, i) for i in range(4)]) for s in (2, 1, 3)]
    bf16 = jnp.bfloat16
    q = lax.axis_index(PLANE).astype(jnp.int32)
    codes = jitter_code.reshape(128, 128)
    dma = pltpu.SemaphoreType.DMA((16,))
    table, head, factor, own = call(
        table_kernel,
        "table",
        48,
        [((16, 256, 1024), bf16), ((2, 256, 1024), bf16), ((32, 8, 256), f32), ((64, 1024), bf16)],
        [SMEM, VMEM, VMEM],
        [pltpu.VMEM((16, 256, 1024), bf16), dma],
        (HBM, VMEM, VMEM, VMEM),
    )(jnp.stack([core, slab_start[0]]), codes, snapshots)
    place = jnp.stack([core, slab_start[0], q])
    table, own, slots, codes, place = lax.optimization_barrier((table, own, slots, codes, place))
    turned, rows = call(
        arrange_kernel,
        "arrange",
        8,
        [((32, 32, 256), bf16), ((256, 1024), bf16)],
        [SMEM] + [VMEM] * 4,
        [pltpu.VMEM((256, 1024), bf16)],
    )(g[None], own, *slots)
    mixed = lax.all_to_all(turned, PLANE, 0, 0, tiled=True)
    keep, give = call(
        partial_kernel,
        "partial",
        48,
        [((16, 512), f32), ((16, 512), f32)],
        [SMEM, VMEM, HBM, VMEM, VMEM],
        [pltpu.VMEM((256, 256), f32)]
        + [pltpu.VMEM((256, 1024), bf16)] * 2
        + [pltpu.VMEM((16, 256, 1024), bf16), dma],
    )(core[None], mixed, table, head, factor)
    keep, give, codes, place = lax.optimization_barrier((keep, give, codes, place))
    other = lax.ppermute(give, "core", swap)
    (norm,) = call(
        norm_kernel,
        "norm",
        8,
        [((16, 128), f32)],
        [SMEM, VMEM],
        [pltpu.VMEM((256, 512), bf16), pltpu.VMEM((16, 512), bf16)],
    )(place, codes)
    (coded,) = call(code_kernel, "code", 8, [((32, 16, 640), jnp.int16)], [VMEM] * 3)(
        keep, other, norm
    )
    half = lax.all_to_all(coded, PLANE, 0, 0, tiled=True)
    half_other = lax.ppermute(half, "core", swap)
    own_part = call(
        own_kernel,
        "own",
        12,
        [((256, 512), f32), ((1, 512), f32), ((16, 128), f32)],
        [SMEM, VMEM, VMEM],
    )(core[None], half, rows)
    steered, gamma_new = call(
        final_kernel,
        "final",
        12,
        [((256, 512), f32), ((1, 512), f32)],
        [SMEM] + [VMEM] * 6 + [SMEM],
    )(core[None], half_other, rows, *own_part, gamma.reshape(1, 512), noise_var)
    return steered, gamma_new.reshape(512)


def solution(mesh):
    fine = Mesh(mesh.devices.reshape(4, 2, 4, 2, 4), ("x", "zl", "y", "core", "grid"))
    sensors = ("x", "zl", "y", "core")
    in_specs = (P((*sensors, "grid"), None), P(), P("grid"), P("grid"), P())
    out_specs = (P(sensors, "grid"), P("grid"))
    return jax.shard_map(on_device, mesh=fine, in_specs=in_specs, out_specs=out_specs, check_vma=False)
```

```python
import jax
import jax.numpy as jnp
import numpy as np
from jax import lax
from jax.experimental import pallas as pl
from jax.experimental.pallas import tpu as pltpu
from jax.sharding import Mesh, PartitionSpec as P

SNAP = 1024
PLANE = ("x", "zl", "y")
NORM_STEPS = 127.9


def fit_sine():
    v = np.cos(np.linspace(0.0, np.pi, 4001)) * 0.25
    basis = np.stack([v ** (2 * i + 1) for i in range(6)], axis=1)
    return tuple(float(c) for c in np.linalg.lstsq(basis, np.sin(2 * np.pi * v), rcond=None)[0])


COEF = fit_sine()


def sine_poly(v):
    w = v * v
    total = jnp.float32(COEF[5])
    for c in COEF[4::-1]:
        total = total * w + jnp.float32(c)
    return total * v


def cos_sin(angle):
    turns = (angle << 10).astype(jnp.float32) * jnp.float32(2.0**-32)
    size = jnp.abs(turns)
    v = size - 0.25
    cosine = -sine_poly(v)
    sine = sine_poly(0.25 - jnp.abs(v))
    return cosine, jnp.where(turns < 0, -sine, sine)


def split(x):
    high = x.astype(jnp.bfloat16)
    return high, (x - high.astype(jnp.float32)).astype(jnp.bfloat16)


def angles(scalars, start_row):
    sub = lax.broadcasted_iota(jnp.int32, (8, 128), 0)
    lane = lax.broadcasted_iota(jnp.int32, (8, 128), 1)
    start = jnp.where(sub == 0, start_row, jnp.where(sub == 1, 1024, 2048))
    return sub, lane + scalars[0] * 256, start, jnp.where(sub == 0, 1 << 15, 0)


def fill_table(pos, constants, table, lanes, lanes_s):
    sub, _, start, keep = constants
    c, s = cos_sin(pos * (sub * 128))
    cc, sc = cos_sin(pos * (sub * 16384))
    ca, sa = cos_sin(pos * start - (pos & 127) * keep)
    c8, s8, c16, s16 = ca[1:2], sa[1:2], ca[2:3], sa[2:3]
    c, s = jnp.concatenate([c, c * c8 - s * s8], axis=0), jnp.concatenate([s, s * c8 + c * s8], axis=0)
    for step in range(8):
        rows = slice(step * 16, step * 16 + 16)
        rows_lo = slice(128 + step * 16, 128 + step * 16 + 16)
        table[rows, lanes], table[rows_lo, lanes] = split(c)
        table[rows, lanes_s], table[rows_lo, lanes_s] = split(s)
        if step < 7:
            c, s = c * c16 - s * s16, s * c16 + c * s16
    return cc, sc, ca[0:1], sa[0:1]


def table_kernel(scalars, jit_ref, rows_ref, table_out, head_ref, factor_ref, own_ref, table_ref, sems):
    own_ref[...] = rows_ref[...]
    constants = angles(scalars, scalars[1])

    def store(b):
        return pltpu.make_async_copy(table_ref.at[b], table_out.at[b], sems.at[b])

    def block(b, carry):
        for part in range(4):
            q = b * 2 + part // 2
            half = part % 2
            cols = slice(half * 128, half * 128 + 128)
            pos = (q * 512 + constants[1] + half * 128) * 64 + jit_ref[pl.ds(q * 4 + scalars[0] * 2 + half, 1), :] + 32
            lanes = slice(part * 128, part * 128 + 128)
            lanes_s = slice(512 + part * 128, 512 + part * 128 + 128)
            cc, sc, ra, rs = fill_table(pos, constants, table_ref.at[b], lanes, lanes_s)
            fc, fs = ra * cc - rs * sc, -(rs * cc + ra * sc)
            factor_ref[q, :, cols] = jnp.concatenate([fc[0:4], fs[0:4]], axis=0)
        store(b).start()
        return carry

    lax.fori_loop(0, 16, block, 0)
    head_ref[...] = table_ref[0:2]
    for b in range(16):
        store(b).wait()


def norm_kernel(scalars, jit_ref, out_ref, table, left):
    constants = angles(scalars, scalars[1])
    q = scalars[2]
    for part in range(2):
        pos = (q * 512 + constants[1] + part * 128) * 64 + jit_ref[pl.ds(q * 4 + scalars[0] * 2 + part, 1), :] + 32
        lanes = slice(part * 128, part * 128 + 128)
        lanes_s = slice(256 + part * 128, 256 + part * 128 + 128)
        cc, sc, ra, rs = fill_table(pos, constants, table, lanes, lanes_s)
        r2, s2 = 2.0 * ra * ra - 1.0, 2.0 * ra * rs
        for value, where in ((r2 * cc - s2 * sc, lanes), (-(s2 * cc + r2 * sc), lanes_s)):
            hi = value.astype(jnp.bfloat16).astype(jnp.float32)
            left[:, where] = jnp.concatenate([hi, value - hi], axis=0).astype(jnp.bfloat16)
    acc = lax.dot_general(left[...], table[...], (((1,), (1,)), ((), ())), preferred_element_type=jnp.float32)
    sums = (acc[0:8, 0:128] + acc[0:8, 128:256]) + (acc[8:16, 0:128] + acc[8:16, 128:256])
    shape = (128, 128)
    column = lax.broadcasted_iota(jnp.int32, shape, 1)
    pick = jnp.where(lax.broadcasted_iota(jnp.int32, shape, 0) == 2 * (column - 64), 1.0, 0.0).astype(jnp.float32)
    even = jnp.dot(sums, pick, precision=lax.Precision.HIGHEST, preferred_element_type=jnp.float32)
    out_ref[0:8] = jnp.round((128.0 + 0.5 * even) * NORM_STEPS)
    out_ref[8:16] = jnp.zeros((8, 128), jnp.float32)


def arrange_kernel(scalars, d0, d2, d1, d3, out_ref, rows_ref, rows):
    g = scalars[0]
    for slot, ref in enumerate((d0, d1, d2, d3)):
        rows[pl.ds(pl.multiple_of(lax.rem(g + slot, 4) * 64, 64), 64), :] = ref[...]
    rows_ref[...] = rows[...]
    for half in range(2):
        turned = rows[:, half * 512 : half * 512 + 512].astype(jnp.float32).T.astype(jnp.bfloat16)
        out_ref[:, half * 16 : half * 16 + 16, :] = turned.reshape(32, 16, 256)


def partial_kernel(scalars, data_ref, table_in, head_ref, factor_ref, keep_ref, give_ref, acc, left0, left1, table_ref, sems):
    dims = (((1,), (1,)), ((), ()))

    def fetch(b):
        return pltpu.make_async_copy(table_in.at[b], table_ref.at[b], sems.at[b])

    for b in range(2, 16):
        fetch(b).start()

    def generate(b, left):
        for part in range(4):
            q = b * 2 + part // 2
            cols = slice(part % 2 * 128, part % 2 * 128 + 128)
            data = data_ref[q, :, cols].astype(jnp.float32)
            lanes = slice(part * 128, part * 128 + 128)
            lanes_s = slice(512 + part * 128, 512 + part * 128 + 128)
            for jh in range(4):
                rows = slice(jh * 32, jh * 32 + 32)
                rows_lo = slice(128 + jh * 32, 128 + jh * 32 + 32)
                left[rows, lanes], left[rows_lo, lanes] = split(data * factor_ref[q, jh : jh + 1, cols])
                left[rows, lanes_s], left[rows_lo, lanes_s] = split(data * factor_ref[q, 4 + jh : 5 + jh, cols])

    def multiply(b, left, tables=table_ref):
        acc[...] += lax.dot_general(left[...], tables[b], dims, preferred_element_type=jnp.float32)

    acc[...] = jnp.zeros_like(acc)
    generate(0, left0)

    def block(i, carry):
        generate(2 * i + 1, left1)
        multiply(2 * i, left0)
        generate(2 * i + 2, left0)
        multiply(2 * i + 1, left1)
        return carry

    generate(1, left1)
    multiply(0, left0, head_ref)
    generate(2, left0)
    multiply(1, left1, head_ref)
    for first, last in ((1, 2), (2, 3), (3, 4), (4, 6), (6, 8)):
        for b in range(2 * first, 2 * last):
            fetch(b).wait()
        lax.fori_loop(first, min(last, 7), block, 0)
    generate(15, left1)
    multiply(14, left0)
    multiply(15, left1)
    first = scalars[0] == 0
    for jh in range(4):
        lanes = slice(jh * 128, jh * 128 + 128)
        row = slice(jh * 32, jh * 32 + 32)
        row_lo = slice(128 + jh * 32, 128 + jh * 32 + 32)
        both = (acc[row, 0:128] + acc[row, 128:256]) + (acc[row_lo, 0:128] + acc[row_lo, 128:256])
        keep_ref[:, lanes] = jnp.where(first, both[0:16], both[16:32])
        give_ref[:, lanes] = jnp.where(first, both[16:32], both[0:16])


def code_kernel(keep_ref, other_ref, norm_ref, out_ref):
    piece = keep_ref[...] + other_ref[...]
    most = jnp.max(jnp.abs(piece), axis=1, keepdims=True)
    power = jnp.ceil(jnp.log2(jnp.maximum(most, 2.0**-60)))
    mantissa = jnp.ceil(most * jnp.exp2(-power) * 16384.0) + 1.0
    unit = mantissa * jnp.exp2(power) * (1.0 / (16384.0 * 32767.0))
    code = jnp.round(piece * (1.0 / unit))
    lane = lax.broadcasted_iota(jnp.int32, (16, 128), 1)
    scale = jnp.where(lane == 0, mantissa, jnp.where(lane == 1, power, norm_ref[...]))
    whole = jnp.concatenate([code, scale], axis=1).astype(jnp.int32).astype(jnp.int16)
    for q in range(32):
        out_ref[q] = whole


def decode(ref):
    scale = ref[:, :, 512:640].astype(jnp.int32).astype(jnp.float32)
    tail = scale.reshape(512, 128)
    unit = tail[:, 0:1] * jnp.exp2(tail[:, 1:2]) * (1.0 / (16384.0 * 32767.0))
    codes = ref[:, :, 0:512].astype(jnp.int32).astype(jnp.float32).reshape(512, 512)
    return codes * unit, jnp.sum(scale, axis=0)


def product(half, ref, data):
    p, tail = decode(ref)
    high, low = split(p * (1.0 / SNAP))
    left = data[:, pl.ds(pl.multiple_of(half * 512, 512), 512)]
    total = jnp.dot(left, high, preferred_element_type=jnp.float32) + jnp.dot(left, low, preferred_element_type=jnp.float32)
    return total, jnp.sum(p * p, axis=0, keepdims=True), tail


def own_kernel(scalars, half_ref, data, out_ref, forms_ref, tail_ref):
    out_ref[...], forms_ref[...], tail_ref[...] = product(scalars[0], half_ref, data)


def final_kernel(scalars, half_ref, data, own_ref, forms_ref, tail_ref, gamma_ref, noise_ref, out_ref, gamma_out):
    total, forms, tails = product(1 - scalars[0], half_ref, data)
    out_ref[...] = own_ref[...] + total
    forms = forms + forms_ref[...]
    tails = tails + tail_ref[...]
    rolled = pltpu.roll(tails, 64, 1)
    below = lax.broadcasted_iota(jnp.int32, (1, 128), 1) < 64
    pieces = [jnp.where(below, rolled[2 * t : 2 * t + 1], tails[2 * t + 1 : 2 * t + 2]) for t in range(4)]
    norms = jnp.concatenate(pieces, axis=1) * (1.0 / NORM_STEPS)
    gamma = gamma_ref[...]
    gamma_out[...] = gamma * (forms * (1.0 / SNAP)) / (norms * (gamma + noise_ref[0]))


VMEM = pl.BlockSpec(memory_space=pltpu.VMEM)
SMEM = pl.BlockSpec(memory_space=pltpu.SMEM)
HBM = pl.BlockSpec(memory_space=pltpu.HBM)


def call(kernel, name, mib, outs, in_specs, scratch=(), out_specs=None):
    return pl.pallas_call(
        kernel,
        out_shape=tuple(jax.ShapeDtypeStruct(*o) for o in outs),
        in_specs=in_specs,
        out_specs=out_specs or (VMEM,) * len(outs),
        scratch_shapes=scratch,
        compiler_params=pltpu.CompilerParams(vmem_limit_bytes=mib * 2**20),
        name=name,
    )


def on_device(snapshots, jitter_code, slab_start, gamma, noise_var):
    core = lax.axis_index("core").astype(jnp.int32)
    g = lax.axis_index("grid").astype(jnp.int32)
    swap = [(0, 1), (1, 0)]
    f32 = jnp.float32
    slots = [lax.ppermute(snapshots, "grid", [((i + s) % 4, i) for i in range(4)]) for s in (2, 1, 3)]
    bf16 = jnp.bfloat16
    q = lax.axis_index(PLANE).astype(jnp.int32)
    codes = jitter_code.reshape(128, 128)
    dma = pltpu.SemaphoreType.DMA((16,))
    table, head, factor, own = call(
        table_kernel,
        "table",
        48,
        [((16, 256, 1024), bf16), ((2, 256, 1024), bf16), ((32, 8, 256), f32), ((64, 1024), bf16)],
        [SMEM, VMEM, VMEM],
        [pltpu.VMEM((16, 256, 1024), bf16), dma],
        (HBM, VMEM, VMEM, VMEM),
    )(jnp.stack([core, slab_start[0]]), codes, snapshots)
    place = jnp.stack([core, slab_start[0], q])
    table, own, slots, codes, place = lax.optimization_barrier((table, own, slots, codes, place))
    turned, rows = call(
        arrange_kernel,
        "arrange",
        8,
        [((32, 32, 256), bf16), ((256, 1024), bf16)],
        [SMEM] + [VMEM] * 4,
        [pltpu.VMEM((256, 1024), bf16)],
    )(g[None], own, *slots)
    mixed = lax.all_to_all(turned, PLANE, 0, 0, tiled=True)
    keep, give = call(
        partial_kernel,
        "partial",
        48,
        [((16, 512), f32), ((16, 512), f32)],
        [SMEM, VMEM, HBM, VMEM, VMEM],
        [pltpu.VMEM((256, 256), f32)]
        + [pltpu.VMEM((256, 1024), bf16)] * 2
        + [pltpu.VMEM((16, 256, 1024), bf16), dma],
    )(core[None], mixed, table, head, factor)
    keep, give, codes, place = lax.optimization_barrier((keep, give, codes, place))
    other = lax.ppermute(give, "core", swap)
    (norm,) = call(
        norm_kernel,
        "norm",
        8,
        [((16, 128), f32)],
        [SMEM, VMEM],
        [pltpu.VMEM((256, 512), bf16), pltpu.VMEM((16, 512), bf16)],
    )(place, codes)
    (coded,) = call(code_kernel, "code", 8, [((32, 16, 640), jnp.int16)], [VMEM] * 3)(
        keep, other, norm
    )
    half = lax.all_to_all(coded, PLANE, 0, 0, tiled=True)
    half_other = lax.ppermute(half, "core", swap)
    own_part = call(
        own_kernel,
        "own",
        12,
        [((256, 512), f32), ((1, 512), f32), ((16, 128), f32)],
        [SMEM, VMEM, VMEM],
    )(core[None], half, rows)
    steered, gamma_new = call(
        final_kernel,
        "final",
        12,
        [((256, 512), f32), ((1, 512), f32)],
        [SMEM] + [VMEM] * 6 + [SMEM],
    )(core[None], half_other, rows, *own_part, gamma.reshape(1, 512), noise_var)
    return steered, gamma_new.reshape(512)


def solution(mesh):
    fine = Mesh(mesh.devices.reshape(4, 2, 4, 2, 4), ("x", "zl", "y", "core", "grid"))
    sensors = ("x", "zl", "y", "core")
    in_specs = (P((*sensors, "grid"), None), P(), P("grid"), P("grid"), P())
    out_specs = (P(sensors, "grid"), P("grid"))
    return jax.shard_map(on_device, mesh=fine, in_specs=in_specs, out_specs=out_specs, check_vma=False)
```
